512 devices in a mesh: inner: 16 (over z_hi, x, core), outer: 32 (over y, z_lo).
Axes of the slice: x: 4, y: 8, z: 8 (z_hi: 2, z_lo: 4; z = z_hi * 4 + z_lo), core: 2. Of those that a mesh axis runs over, the one named last changes fastest.
Arguments:
- acts: bfloat16 [65536, 8192], P(('inner', 'outer')), may hold values from -24 to 24
- cotangent: bfloat16 [65536, 8192], P(('inner', 'outer')), may hold values from -0.75 to 0.75
- latent_ids: int32 [65536, 4], P(('inner', 'outer')), may hold values from 0 to 255, all different within a row
- enc_rows: bfloat16 [256, 8192], P('inner'), may hold values from -0.0625 to 0.0625
- dec_rows: bfloat16 [256, 8192], P('inner'), may hold values from -0.0625 to 0.0625
Outputs:
- enc_grad: float32 [256, 8192], P('outer', 'inner')
- dec_grad: float32 [256, 8192], P('outer', 'inner')
The draws below stay inside these ranges and needn't reach their ends.
Inputs may be any that keep to these rules, and one draw needn't show every extreme that they name: `latent_ids`: each row names 4 different latents; every latent is named by some row.
All inputs are finite; a program needn't handle non-finite values.
Results may differ from the reference program's by a relative error of at most 0.0095.
Values may be sent and summed in bfloat16 or wider, within the bound.
A program may use at most 64 MiB of HBM per device.

```python
import jax
import jax.numpy as jnp
from jax import lax

D = 8192
LB = 256
TOK_DEV = 128
K = 4
TOKENS = 65536
N_INNER = 16
N_OUTER = 32


def with_spikes(entries, own_key, source, target, blocks, factor):
    owner, partner = [(jnp.arange(entries.shape[axis_at]) // (entries.shape[axis_at] // blocks)).reshape([-1 if axis == axis_at else 1 for axis in range(entries.ndim)]) for axis_at in (source, target)]
    chosen = jax.random.permutation(own_key, blocks)[partner]
    strong = (owner == chosen) | (owner == (partner + blocks // 2) % blocks)
    return jnp.where(strong, factor * entries, entries)


def block_levels(rng, dims, pieces, least, top_value):
    loudness, own = 1.0, jax.random.fold_in(rng, 6)
    for axis_at, shards_of in pieces:
        steps = jnp.exp(jax.random.uniform(jax.random.fold_in(own, axis_at), (shards_of,), jnp.float32, least / len(pieces), top_value / len(pieces)))
        loudness = loudness * jnp.repeat(steps, dims[axis_at] // shards_of).reshape([-1 if axis == axis_at else 1 for axis in range(len(dims))])
    return loudness


def picks_of(rng, rows, number_of, top, lift):
    ranking = jax.random.permutation(jax.random.fold_in(rng, 1), number_of)
    pull = ranking
    for power in range(3):
        pull = pull * pull // number_of
    pull = pull * lift // number_of
    tickets = jax.random.randint(jax.random.fold_in(rng, 2), (rows, number_of), 0, 4096) + pull
    sure = jax.random.permutation(jax.random.fold_in(rng, 3), rows)[jnp.arange(number_of) % rows]
    tickets = jnp.where(jnp.arange(rows)[:, None] == sure[None, :], 1 << 14, tickets)
    merit = tickets * number_of + jnp.arange(number_of)
    return lax.top_k(merit.astype(jnp.int32), top)[1].astype(jnp.int32)


def normal_values(stream_key, shape, scale, reach, shards=(), held_as=jnp.bfloat16):
    level = block_levels(stream_key, shape, shards, -0.22, 0.18) if shards else 1.0
    drawn = jax.random.normal(stream_key, shape, jnp.float32) * scale * level
    return jnp.minimum(jnp.maximum(drawn, -reach), reach).astype(held_as)


def heavy_noise(key, shape, width, reach, shards, heavy, kind=jnp.bfloat16):
    drawn = width * jax.random.normal(key, shape, jnp.float32)
    if shards:
        drawn = drawn * block_levels(key, shape, shards, -0.22, 0.18)
    return jnp.clip(with_spikes(drawn, jax.random.fold_in(key, 3), *heavy), -reach, reach).astype(kind)


def setup_inputs(seed: int = 0) -> dict:
    streams_of = jax.random.split(jax.random.key(seed), 6)
    return {
        "acts": heavy_noise(streams_of[0], (TOKENS, D), 1.0, 24.0, ((0, 512),), (0, 1, 512, 6.0)),
        "cotangent": heavy_noise(streams_of[1], (TOKENS, D), ((TOKENS * K / LB) ** -0.5), 0.75, ((0, 512),), (0, 1, 512, 6.0)),
        "latent_ids": picks_of(streams_of[2], TOKENS, LB, K, 128),
        "enc_rows": normal_values(streams_of[3], (LB, D), D ** -0.5, 0.0625, ((0, 16),)),
        "dec_rows": normal_values(streams_of[4], (LB, D), D ** -0.5, 0.0625, ((0, 16),)),
    }


def narrow(term):
    return lax.optimization_barrier(term.astype(jnp.bfloat16)).astype(jnp.float32)


def device_term(tok_acts, tok_cot, tok_ids, enc_rows, dec_rows):
    latents = jnp.arange(LB, dtype=jnp.int32)
    mask = jnp.any(tok_ids[:, :, None] == latents[None, None, :], axis=1).astype(jnp.float32)
    pre = jnp.dot(tok_acts, enc_rows.T, preferred_element_type=jnp.float32)
    codes = (pre * mask).astype(jnp.bfloat16)
    back = jnp.dot(tok_cot, dec_rows.T, preferred_element_type=jnp.float32)
    dcodes = (back * mask).astype(jnp.bfloat16)
    term_enc = jnp.dot(dcodes.T, tok_acts, preferred_element_type=jnp.float32)
    term_dec = jnp.dot(codes.T, tok_cot, preferred_element_type=jnp.float32)
    return jnp.stack([term_enc, term_dec])


def reference(acts, cotangent, latent_ids, enc_rows, dec_rows):
    def group_sum(outer_idx):
        def add_device(inner_idx, total):
            start = ((inner_idx * N_OUTER + outer_idx) * TOK_DEV).astype(jnp.int32)
            tok_acts = lax.dynamic_slice_in_dim(acts, start, TOK_DEV, 0)
            tok_cot = lax.dynamic_slice_in_dim(cotangent, start, TOK_DEV, 0)
            tok_ids = lax.dynamic_slice_in_dim(latent_ids, start, TOK_DEV, 0)
            return total + narrow(device_term(tok_acts, tok_cot, tok_ids, enc_rows, dec_rows))

        section_sum = lax.fori_loop(0, N_INNER, add_device, jnp.zeros((2, LB, D), jnp.float32))
        return narrow(section_sum)

    total = lax.fori_loop(0, N_OUTER, lambda outer_idx, accum: accum + group_sum(outer_idx),
                          jnp.zeros((2, LB, D), jnp.float32))
    return total[0], total[1]
```

```python
import functools

import jax
import jax.numpy as jnp
from jax import lax
from jax.experimental import pallas as pl
from jax.experimental.pallas import tpu as pltpu
from jax.sharding import PartitionSpec as P

MESH = pl.DeviceIdType.MESH
PIECES = 2
NX, NY, NZ, NZL = 4, 8, 8, 4
GROUP = 16
CUBES = 32
TOK, LB, BLOCK = 128, 256, 512
K = 4


def div(a, b):
    return lax.div(jnp.int32(a), jnp.int32(b))


def rem(a, b):
    return lax.rem(jnp.int32(a), jnp.int32(b))


def place():
    inner, outer = lax.axis_index("inner"), lax.axis_index("outer")
    zh, x, c = div(inner, 8), rem(div(inner, 2), 4), rem(inner, 2)
    y, zl = div(outer, 4), rem(outer, 4)
    return x, y, zh * 4 + zl, c


def device(x, y, z, c):
    return (div(z, 4) * 8 + x * 2 + c, y * 4 + rem(z, 4))


def block_of(x, y, z, c):
    return rem(z, 2) * 8 + rem(y, 2) * 4 + rem(x, 2) * 2 + c


def step(v, s):
    return (1 - 2 * rem(v, 2)) * (1 - 2 * s)


def peer(s, d):
    x, y, z, c = place()
    dx, dy, dz, dc = div(d, 8), rem(div(d, 4), 2), rem(div(d, 2), 2), rem(d, 2)
    return (
        rem(x + dx * step(x, s) + NX, NX),
        rem(y + dy * step(y, s) + NY, NY),
        rem(z + dz * step(z, s) + NZ, NZ),
        rem(c + dc, 2),
    )


def kernel(acts, cot, ids, enc, dec, oenc, odec,
           tok, rows, idsb, pout, pin, cout, cin, spread, tsend, fin,
           tok_s, tok_r, row_s, row_r, ids_s, ids_r, p_s, p_r, c_s, c_r, f_s, f_r):
    W = BLOCK // PIECES
    x, y, z, c = place()
    inner = lax.axis_index("inner")
    me = device(x, y, z, c)
    mine = block_of(x, y, z, c)
    zl = rem(z, 4)

    def inner_peer(e):
        i = rem(inner + e, 16)
        return i, (i, y * 4 + zl)

    def source(k):
        x1 = 2 * div(k, 16) + rem(x, 2)
        y1 = 2 * rem(div(k, 4), 4) + div(x, 2)
        z1 = 2 * rem(k, 4) + div(z, 4)
        return device(x1, y1, z1, c)

    barrier = pltpu.get_barrier_semaphore()

    @pl.loop(1, GROUP)
    def _(d):
        for s in range(PIECES):
            pl.semaphore_signal(barrier, inc=1, device_id=device(*peer(s, d)), device_id_type=MESH)
        pl.semaphore_signal(barrier, inc=1, device_id=inner_peer(d)[1], device_id_type=MESH)

    @pl.loop(0, CUBES)
    def _(k):
        src = source(k)

        @pl.when((src[0] != me[0]) | (src[1] != me[1]))
        def _():
            pl.semaphore_signal(barrier, inc=1, device_id=src, device_id_type=MESH)

    stays = (rem(z, 2) == div(z, 4)) & (rem(y, 2) * 2 + rem(x, 2) == x)
    pl.semaphore_wait(barrier, (GROUP - 1) * (PIECES + 1) + CUBES - stays.astype(jnp.int32))

    def columns(block, s):
        return pl.ds(pl.multiple_of(block * BLOCK + s * W, W), W)

    def ids_copy(s, d):
        return pltpu.make_async_remote_copy(
            src_ref=ids, dst_ref=idsb.at[s, d], send_sem=ids_s.at[s, d], recv_sem=ids_r.at[s, d],
            device_id=device(*peer(s, d)), device_id_type=MESH)

    def tok_copy(a, s, d):
        p = peer(s, d)
        return pltpu.make_async_remote_copy(
            src_ref=(acts, cot)[a].at[:, columns(block_of(*p), s)], dst_ref=tok.at[a, s, d],
            send_sem=tok_s.at[a, s, d], recv_sem=tok_r.at[a, s, d],
            device_id=device(*p), device_id_type=MESH)

    def own_tok(a, s):
        return pltpu.make_async_copy(
            (acts, cot)[a].at[:, columns(mine, s)], tok.at[a, s, 0], tok_r.at[a, s, 0])

    def row_copy(a, e):
        i, dev = inner_peer(e)
        block = rem(z, 2) * 8 + rem(y, 2) * 4 + rem(div(i, 2), 2) * 2 + rem(i, 2)
        return pltpu.make_async_remote_copy(
            src_ref=(enc, dec)[a].at[:, pl.ds(pl.multiple_of(block * BLOCK, BLOCK), BLOCK)],
            dst_ref=rows.at[a, pl.ds(pl.multiple_of(inner * 16, 16), 16), :],
            send_sem=row_s.at[a, e], recv_sem=row_r.at[a, e], device_id=dev, device_id_type=MESH)

    def own_row(a):
        return pltpu.make_async_copy(
            (enc, dec)[a].at[:, pl.ds(pl.multiple_of(mine * BLOCK, BLOCK), BLOCK)],
            rows.at[a, pl.ds(pl.multiple_of(inner * 16, 16), 16), :], row_r.at[a, 0])

    def part_copy(s, d):
        return pltpu.make_async_remote_copy(
            src_ref=pout.at[s, d], dst_ref=pin.at[s, d], send_sem=p_s.at[s, d], recv_sem=p_r.at[s, d],
            device_id=device(*peer(s, d)), device_id_type=MESH)

    def code_copy(s, d):
        return pltpu.make_async_remote_copy(
            src_ref=cout, dst_ref=cin.at[s, d], send_sem=c_s.at[s, d], recv_sem=c_r.at[s, d],
            device_id=device(*peer(s, d)), device_id_type=MESH)

    cube = div(x, 2) * 16 + div(y, 2) * 4 + div(z, 2)

    def final_dest(j):
        return (rem(z, 2) * 8 + (rem(y, 2) * 2 + rem(x, 2)) * 2 + c,
                rem(y + div(j, 4), 8) * 4 + rem(zl + rem(j, 4), 4))

    def final_copy(j):
        dev = final_dest(j)
        return pltpu.make_async_remote_copy(
            src_ref=tsend.at[dev[1]], dst_ref=fin.at[cube], send_sem=f_s.at[j], recv_sem=f_r.at[cube],
            device_id=dev, device_id_type=MESH)

    def own_final():
        return pltpu.make_async_copy(tsend.at[me[1]], fin.at[cube], f_s.at[0])

    for a in range(2):
        own_row(a).start()

    @pl.loop(1, 16)
    def _(e):
        for a in range(2):
            row_copy(a, e).start()
        for s in range(PIECES):
            ids_copy(s, e).start()

    for a in range(2):
        for s in range(PIECES):
            own_tok(a, s).start()

    @pl.loop(1, GROUP)
    def _(d):
        for s in range(PIECES):
            for a in range(2):
                tok_copy(a, s, d).start()

    for s in range(PIECES):
        idsb[s, 0] = ids[...]

    for a in range(2):
        own_row(a).wait()

    @pl.loop(1, 16)
    def _(e):
        for a in range(2):
            row_copy(a, e).wait_recv()

    latent = lax.broadcasted_iota(jnp.int32, (LB, TOK), 0)

    def partial(s, d):
        which = idsb[s, d]
        out = []
        for a in range(2):
            full = lax.dot_general(rows[a, :, s * W:(s + 1) * W], tok[a, s, d],
                                   (((1,), (1,)), ((), ())), preferred_element_type=jnp.float32)
            for k in range(K):
                out.append(jnp.sum(jnp.where(which[k:k + 1, :] == latent, full, 0.0), axis=0, keepdims=True))
        return jnp.concatenate(out, axis=0)

    for s in range(PIECES):
        for a in range(2):
            own_tok(a, s).wait()
        pin[s, 0] = partial(s, 0)

    @pl.loop(1, GROUP)
    def _(d):
        for s in range(PIECES):
            ids_copy(s, d).wait_recv()
            for a in range(2):
                tok_copy(a, s, d).wait_recv()
            pout[s, d] = partial(s, d)
            part_copy(s, d).start()

    @pl.loop(1, GROUP)
    def _(d):
        for s in range(PIECES):
            part_copy(s, d).wait_recv()

    codes = jnp.zeros((2 * K, TOK), jnp.float32)
    for s in range(PIECES):
        for d in range(GROUP):
            codes = codes + pin[s, d]
    cout[...] = codes.astype(jnp.bfloat16).astype(jnp.float32)

    @pl.loop(1, GROUP)
    def _(d):
        for s in range(PIECES):
            code_copy(s, d).start()

    for s in range(PIECES):
        cin[s, 0] = cout[...]

    def expand(s, d):
        which, values = idsb[s, d], cin[s, d]
        at = pl.ds(pl.multiple_of(d * TOK, TOK), TOK)
        for a in range(2):
            full = jnp.zeros((LB, TOK), jnp.float32)
            for k in range(K):
                full = jnp.where(which[k:k + 1, :] == latent, values[a * K + k:a * K + k + 1, :], full)
            spread[a, s, :, at] = full.astype(jnp.bfloat16)

    for s in range(PIECES):
        expand(s, 0)

    @pl.loop(1, GROUP)
    def _(d):
        for s in range(PIECES):
            code_copy(s, d).wait_recv()
            expand(s, d)

    for s in range(PIECES):
        terms = []
        for a in range(2):
            right = tok[a, s].reshape(GROUP * TOK, W)
            terms.append(lax.dot_general(spread[1 - a, s], right, (((1,), (0,)), ((), ())),
                                         preferred_element_type=jnp.float32).reshape(CUBES, 8, W))
        tsend[:, :, s * W:(s + 1) * W] = jnp.concatenate(terms, axis=1).astype(jnp.bfloat16)

    @pl.when(stays)
    def _():
        own_final().start()

    @pl.when(jnp.logical_not(stays))
    def _():
        final_copy(0).start()

    @pl.loop(1, CUBES)
    def _(j):
        final_copy(j).start()

    @pl.loop(1, GROUP)
    def _(d):
        for a in range(2):
            row_copy(a, d).wait_send()
        for s in range(PIECES):
            ids_copy(s, d).wait_send()
            part_copy(s, d).wait_send()
            code_copy(s, d).wait_send()
            for a in range(2):
                tok_copy(a, s, d).wait_send()

    @pl.when(stays)
    def _():
        own_final().wait()

    @pl.when(jnp.logical_not(stays))
    def _():
        final_copy(0).wait_send()

    @pl.loop(1, CUBES)
    def _(j):
        final_copy(j).wait_send()

    @pl.loop(0, CUBES)
    def _(k):
        @pl.when(jnp.logical_not(stays & (k == cube)))
        def _():
            pltpu.make_async_remote_copy(
                src_ref=tsend.at[0], dst_ref=fin.at[k], send_sem=f_s.at[0], recv_sem=f_r.at[k],
                device_id=me, device_id_type=MESH).wait_recv()

    total = jnp.zeros((16, BLOCK), jnp.float32)
    for k in range(CUBES):
        total = total + fin[k].astype(jnp.float32)
    oenc[...] = total[:8]
    odec[...] = total[8:]


def local(acts, cotangent, latent_ids, enc_rows, dec_rows):
    S, W = PIECES, BLOCK // PIECES
    ids = latent_ids.T
    ids = jnp.concatenate([ids, ids], axis=0)
    vmem, hbm = pl.BlockSpec(memory_space=pltpu.VMEM), pl.BlockSpec(memory_space=pl.ANY)
    dma = pltpu.SemaphoreType.DMA
    return pl.pallas_call(
        kernel,
        out_shape=(jax.ShapeDtypeStruct((8, BLOCK), jnp.float32),) * 2,
        in_specs=[hbm, hbm, vmem, hbm, hbm],
        out_specs=(vmem, vmem),
        scratch_shapes=[
            pltpu.VMEM((2, S, GROUP, TOK, W), jnp.bfloat16),
            pltpu.VMEM((2, LB, BLOCK), jnp.bfloat16),
            pltpu.VMEM((S, GROUP, 8, TOK), jnp.int32),
            pltpu.VMEM((S, GROUP, 8, TOK), jnp.float32),
            pltpu.VMEM((S, GROUP, 8, TOK), jnp.float32),
            pltpu.VMEM((8, TOK), jnp.float32),
            pltpu.VMEM((S, GROUP, 8, TOK), jnp.float32),
            pltpu.VMEM((2, S, LB, GROUP * TOK), jnp.bfloat16),
            pltpu.VMEM((CUBES, 16, BLOCK), jnp.bfloat16),
            pltpu.VMEM((CUBES, 16, BLOCK), jnp.bfloat16),
            dma((2, S, GROUP)), dma((2, S, GROUP)),
            dma((2, 16)), dma((2, 16)),
            dma((S, GROUP)), dma((S, GROUP)),
            dma((S, GROUP)), dma((S, GROUP)),
            dma((S, GROUP)), dma((S, GROUP)),
            dma((CUBES,)), dma((CUBES,)),
        ],
        compiler_params=pltpu.CompilerParams(
            collective_id=0, has_side_effects=True, vmem_limit_bytes=40 * 2**20),
    )(acts, cotangent, ids, enc_rows, dec_rows)


def solution(mesh):
    placed = (
        P(("inner", "outer"), None),
        P(("inner", "outer"), None),
        P(("inner", "outer"), None),
        P("inner", None),
        P("inner", None),
    )
    return jax.shard_map(
        local,
        mesh=mesh,
        in_specs=placed,
        out_specs=(P("outer", "inner"), P("outer", "inner")),
        check_vma=False,
    )
```

```python
import functools

import jax
import jax.numpy as jnp
from jax import lax
from jax.experimental import pallas as pl
from jax.experimental.pallas import tpu as pltpu
from jax.sharding import PartitionSpec as P

MESH = pl.DeviceIdType.MESH
PIECES = 2
NX, NY, NZ = 4, 8, 8
GROUP = 16
CUBES = 32
TOK, LB, BLOCK = 128, 256, 512
K = 4
PEERS = sorted(range(1, GROUP), key=lambda d: (-bin(d >> 1).count("1"), d))


def div(a, b):
    return lax.div(a, jnp.int32(b))


def rem(a, b):
    return lax.rem(a, jnp.int32(b))


def towards(v, s, n):
    return rem(v + (1 - 2 * rem(v, 2)) * (1 - 2 * s) + n, n)


def kernel(acts, cot, ids, enc, dec, oenc, odec,
           tok, rows, idsb, pout, pin, cout, cin, spread, tsend, fin,
           tok_s, tok_r, row_s, row_r, ids_s, ids_r, p_s, p_r, c_s, c_r, f_s, f_r):
    W = BLOCK // PIECES
    inner, outer = lax.axis_index("inner"), lax.axis_index("outer")
    zh, x, c = div(inner, 8), rem(div(inner, 2), 4), rem(inner, 2)
    y, zl = div(outer, 4), rem(outer, 4)
    z = zh * 4 + zl
    me = (inner, outer)
    px, py, pz = rem(x, 2), rem(y, 2), rem(z, 2)
    pieces = range(PIECES)

    cs = (c, 1 - c)
    x2 = [(x * 2, towards(x, s, NX) * 2) for s in pieces]
    y4 = [(y * 4, towards(y, s, NY) * 4) for s in pieces]
    zz = [(z, towards(z, s, NZ)) for s in pieces]
    z8 = [tuple(div(v, 4) * 8 for v in pair) for pair in zz]
    zr = [tuple(rem(v, 4) for v in pair) for pair in zz]
    xc = [[[x2[s][dx] + cs[dc] for dc in range(2)] for dx in range(2)] for s in pieces]
    bx, by, bz = (px * 2, 2 - px * 2), (py * 4, 4 - py * 4), (pz * 8, 8 - pz * 8)
    bxc = [[bx[dx] + cs[dc] for dc in range(2)] for dx in range(2)]
    byz = [[by[dy] + bz[dz] for dz in range(2)] for dy in range(2)]

    def bits(d):
        return d >> 3, (d >> 2) & 1, (d >> 1) & 1, d & 1

    def peer(s, d):
        dx, dy, dz, dc = bits(d)
        return z8[s][dz] + xc[s][dx][dc], y4[s][dy] + zr[s][dz]

    def block(d):
        dx, dy, dz, dc = bits(d)
        return bxc[dx][dc] + byz[dy][dz]

    inner_at = [inner] + [rem(inner + e, 16) for e in range(1, 16)]

    def inner_block(e):
        return rem(inner_at[e], 4) + byz[0][0]

    mx, my = px, div(x, 2)
    src_x = [(2 * kx + mx) * 2 + c for kx in range(2)]
    src_y = [(2 * ky + my) * 4 for ky in range(4)]
    src_z = [2 * kz + zh for kz in range(4)]
    src_z = [(div(v, 4) * 8, rem(v, 4)) for v in src_z]
    dest_inner = pz * 8 + (py * 2 + px) * 2 + c
    dest_y = [rem(y + dy, NY) * 4 for dy in range(NY)]
    dest_z = [rem(zl + dz, 4) for dz in range(4)]
    dests = [dest_y[dy] + dest_z[dz] for dy in range(NY) for dz in range(4)]
    cube = div(x, 2) * 16 + div(y, 2) * 4 + div(z, 2)
    stays = dest_inner == inner

    barrier = pltpu.get_barrier_semaphore()
    for d in range(1, GROUP):
        for s in pieces:
            pl.semaphore_signal(barrier, inc=1, device_id=peer(s, d), device_id_type=MESH)
        pl.semaphore_signal(barrier, inc=1, device_id=(inner_at[d], outer), device_id_type=MESH)
    for kx in range(2):
        for ky in range(4):
            for kz in range(4):
                src = (src_z[kz][0] + src_x[kx], src_y[ky] + src_z[kz][1])

                @pl.when((src[0] != inner) | (src[1] != outer))
                def _():
                    pl.semaphore_signal(barrier, inc=1, device_id=src, device_id_type=MESH)

    pl.semaphore_wait(barrier, (GROUP - 1) * (PIECES + 1) + CUBES - stays.astype(jnp.int32))

    def remote(src, dst, send, recv, dev):
        return pltpu.make_async_remote_copy(
            src_ref=src, dst_ref=dst, send_sem=send, recv_sem=recv, device_id=dev, device_id_type=MESH)

    def arrived(ref, sem):
        pltpu.make_async_copy(ref, ref, sem).wait()

    def columns(at, width):
        return pl.ds(pl.multiple_of(at, width), width)

    row_slot = pl.ds(pl.multiple_of(inner * 16, 16), 16)

    for a in range(2):
        pltpu.make_async_copy(
            (enc, dec)[a].at[:, columns(block(0) * BLOCK, BLOCK)], rows.at[a, row_slot, :], row_r).start()
    for e in range(1, 16):
        for a in range(2):
            remote((enc, dec)[a].at[:, columns(inner_block(e) * BLOCK, BLOCK)], rows.at[a, row_slot, :],
                   row_s, row_r, (inner_at[e], outer)).start()
    for d in PEERS:
        for s in pieces:
            for a in range(2):
                remote((acts, cot)[a].at[:, columns(block(d) * BLOCK + s * W, W)], tok.at[a, s, d],
                       tok_s, tok_r.at[a, s, d], peer(s, d)).start()
        for s in pieces:
            remote(ids, idsb.at[s, d], ids_s, ids_r, peer(s, d)).start()
    for s in pieces:
        for a in range(2):
            pltpu.make_async_copy((acts, cot)[a].at[:, columns(block(0) * BLOCK + s * W, W)],
                                  tok.at[a, s, 0], tok_r.at[a, s, 0]).start()
        idsb[s, 0] = ids[...]

    latent = lax.broadcasted_iota(jnp.int32, (LB, 2 * TOK), 0)

    def both(ref, s, d):
        return jnp.concatenate([ref[s, d], ref[s, d + 1]], axis=1)

    def partial(s, d):
        which = both(idsb, s, d)
        hits = [which[k:k + 1, :] == latent for k in range(K)]
        out = []
        for a in range(2):
            full = lax.dot_general(rows[a, :, s * W:(s + 1) * W], tok[a, s, d:d + 2].reshape(2 * TOK, W),
                                   (((1,), (1,)), ((), ())), preferred_element_type=jnp.float32)
            for k in range(K):
                out.append(jnp.sum(jnp.where(hits[k], full, 0.0), axis=0, keepdims=True))
        out = jnp.concatenate(out, axis=0)
        return out[:, :TOK], out[:, TOK:]

    others = pl.ds(1, GROUP - 1)
    arrived(rows, row_r)
    arrived(idsb.at[:, others], ids_r)
    order = []
    for d in PEERS:
        if d & ~1 not in order and d & ~1:
            order.append(d & ~1)
    for d in order + [0]:
        for s in pieces:
            for one in (d, d + 1):
                for a in range(2):
                    arrived(tok.at[a, s, one], tok_r.at[a, s, one])
            for one, value in zip((d, d + 1), partial(s, d)):
                if one == 0:
                    pin[s, 0] = value
                else:
                    pout[s, one] = value
                    remote(pout.at[s, one], pin.at[s, one], p_s, p_r, peer(s, one)).start()

    arrived(rows.at[:, pl.ds(0, LB - 16), :], row_s)
    arrived(idsb.at[:, others], ids_s)
    arrived(tok.at[:, :, others], tok_s)

    arrived(pin.at[:, others], p_r)
    codes = jnp.sum(pin[...].reshape(PIECES * GROUP, 2 * K, TOK), axis=0)
    cout[...] = codes.astype(jnp.bfloat16).astype(jnp.float32)
    for d in PEERS:
        for s in pieces:
            remote(cout, cin.at[s, d], c_s, c_r, peer(s, d)).start()
    for s in pieces:
        cin[s, 0] = cout[...]
    arrived(pout.at[:, others], p_s)
    arrived(cin.at[:, others], c_r)

    for s in pieces:
        for d in range(0, GROUP, 2):
            which, values = both(idsb, s, d), both(cin, s, d)
            hits = [which[k:k + 1, :] == latent for k in range(K)]
            for a in range(2):
                full = jnp.zeros((LB, 2 * TOK), jnp.float32)
                for k in range(K):
                    full = jnp.where(hits[k], values[a * K + k:a * K + k + 1, :], full)
                spread[a, s, :, d * TOK:(d + 2) * TOK] = full.astype(jnp.bfloat16)
        terms = []
        for a in range(2):
            terms.append(lax.dot_general(spread[1 - a, s], tok[a, s].reshape(GROUP * TOK, W),
                                         (((1,), (0,)), ((), ())),
                                         preferred_element_type=jnp.float32).reshape(CUBES, 8, W))
        tsend[:, :, s * W:(s + 1) * W] = jnp.concatenate(terms, axis=1).astype(jnp.bfloat16)

    @pl.when(stays)
    def _():
        pltpu.make_async_copy(tsend.at[outer], fin.at[cube], f_r).start()

    @pl.when(jnp.logical_not(stays))
    def _():
        remote(tsend.at[outer], fin.at[cube], f_s, f_r, (dest_inner, outer)).start()

    for at in dests[1:]:
        remote(tsend.at[at], fin.at[cube], f_s, f_r, (dest_inner, at)).start()
    arrived(cin.at[:, others], c_s)
    arrived(fin, f_r)
    total = jnp.zeros((16, BLOCK), jnp.float32)
    for k in range(CUBES):
        total = total + fin[k].astype(jnp.float32)
    oenc[...] = total[:8]
    odec[...] = total[8:]

    @pl.when(stays)
    def _():
        arrived(tsend.at[pl.ds(1, CUBES - 1)], f_s)

    @pl.when(jnp.logical_not(stays))
    def _():
        arrived(tsend, f_s)


def local(acts, cotangent, latent_ids, enc_rows, dec_rows):
    S, W = PIECES, BLOCK // PIECES
    ids = latent_ids.T
    ids = jnp.concatenate([ids, ids], axis=0)
    vmem, hbm = pl.BlockSpec(memory_space=pltpu.VMEM), pl.BlockSpec(memory_space=pl.ANY)
    dma = pltpu.SemaphoreType.DMA
    return pl.pallas_call(
        kernel,
        out_shape=(jax.ShapeDtypeStruct((8, BLOCK), jnp.float32),) * 2,
        in_specs=[hbm, hbm, vmem, hbm, hbm],
        out_specs=(vmem, vmem),
        scratch_shapes=[
            pltpu.VMEM((2, S, GROUP, TOK, W), jnp.bfloat16),
            pltpu.VMEM((2, LB, BLOCK), jnp.bfloat16),
            pltpu.VMEM((S, GROUP, 8, TOK), jnp.int32),
            pltpu.VMEM((S, GROUP, 8, TOK), jnp.float32),
            pltpu.VMEM((S, GROUP, 8, TOK), jnp.float32),
            pltpu.VMEM((8, TOK), jnp.float32),
            pltpu.VMEM((S, GROUP, 8, TOK), jnp.float32),
            pltpu.VMEM((2, S, LB, GROUP * TOK), jnp.bfloat16),
            pltpu.VMEM((CUBES, 16, BLOCK), jnp.bfloat16),
            pltpu.VMEM((CUBES, 16, BLOCK), jnp.bfloat16),
            dma, dma((2, S, GROUP)),
            dma, dma, dma, dma, dma, dma, dma, dma, dma, dma,
        ],
        compiler_params=pltpu.CompilerParams(
            collective_id=0, has_side_effects=True, vmem_limit_bytes=60 * 2**20),
    )(acts, cotangent, ids, enc_rows, dec_rows)


def solution(mesh):
    placed = (
        P(("inner", "outer"), None),
        P(("inner", "outer"), None),
        P(("inner", "outer"), None),
        P("inner", None),
        P("inner", None),
    )
    return jax.shard_map(
        local,
        mesh=mesh,
        in_specs=placed,
        out_specs=(P("outer", "inner"), P("outer", "inner")),
        check_vma=False,
    )
```

```python
import functools

import jax
import jax.numpy as jnp
from jax import lax
from jax.experimental import pallas as pl
from jax.experimental.pallas import tpu as pltpu
from jax.sharding import PartitionSpec as P

MESH = pl.DeviceIdType.MESH
PIECES = 2
NX, NY, NZ = 4, 8, 8
GROUP = 16
CUBES = 32
CHIPS = 8
WINDOW = 8
TOK, LB, BLOCK = 128, 256, 512
K = 4
PEERS = sorted(range(1, GROUP), key=lambda d: (-bin(d >> 1).count("1"), d))


def div(a, b):
    return lax.div(a, jnp.int32(b))


def rem(a, b):
    return lax.rem(a, jnp.int32(b))


def towards(v, s, n):
    return rem(v + (1 - 2 * rem(v, 2)) * (1 - 2 * s) + n, n)


def kernel(acts, cot, ids, enc, dec, oenc, odec,
           tok, rows, idsb, pout, pin, cout, cin, spread, tsend, fin,
           tok_s, tok_r, row_s, row_r, cross_s, cross_r, relay_s, ids_s, ids_r, p_s, p_r, c_s, c_r, f_s, f_r):
    W = BLOCK // PIECES
    inner, outer = lax.axis_index("inner"), lax.axis_index("outer")
    zh, x, c = div(inner, 8), rem(div(inner, 2), 4), rem(inner, 2)
    y, zl = div(outer, 4), rem(outer, 4)
    z = zh * 4 + zl
    me = (inner, outer)
    px, py, pz = rem(x, 2), rem(y, 2), rem(z, 2)
    pieces = range(PIECES)

    cs = (c, 1 - c)
    x2 = [(x * 2, towards(x, s, NX) * 2) for s in pieces]
    y4 = [(y * 4, towards(y, s, NY) * 4) for s in pieces]
    zz = [(z, towards(z, s, NZ)) for s in pieces]
    z8 = [tuple(div(v, 4) * 8 for v in pair) for pair in zz]
    zr = [tuple(rem(v, 4) for v in pair) for pair in zz]
    xc = [[[x2[s][dx] + cs[dc] for dc in range(2)] for dx in range(2)] for s in pieces]
    bx, by, bz = (px * 2, 2 - px * 2), (py * 4, 4 - py * 4), (pz * 8, 8 - pz * 8)
    bxc = [[bx[dx] + cs[dc] for dc in range(2)] for dx in range(2)]
    byz = [[by[dy] + bz[dz] for dz in range(2)] for dy in range(2)]

    def bits(d):
        return d >> 3, (d >> 2) & 1, (d >> 1) & 1, d & 1

    def peer(s, d):
        dx, dy, dz, dc = bits(d)
        return z8[s][dz] + xc[s][dx][dc], y4[s][dy] + zr[s][dz]

    def block(d):
        dx, dy, dz, dc = bits(d)
        return bxc[dx][dc] + byz[dy][dz]

    half = zh * 8
    beside = [half + rem(rem(inner, 8) + e, 8) for e in range(8)]
    across = [8 - half + i for i in range(8)]
    border = (zl == 0) | (zl == 3)
    facing = y * 4 + 3 - zl
    further = y * 4 + rem(zl + 2, 4)

    mx, my = px, div(x, 2)
    src_x = [(2 * kx + mx) * 2 + c for kx in range(2)]
    src_y = [(2 * ky + my) * 4 for ky in range(4)]
    src_z = [2 * kz + zh for kz in range(4)]
    src_z = [(div(v, 4) * 8, rem(v, 4)) for v in src_z]
    dest_inner = pz * 8 + (py * 2 + px) * 2 + c
    dest_y = [rem(y + dy, NY) * 4 for dy in range(NY)]
    dest_z = [rem(zl + dz, 4) for dz in range(4)]
    dests = [dest_y[dy] + dest_z[dz] for dy in range(NY) for dz in range(4)]
    cube = div(x, 2) * 16 + div(y, 2) * 4 + div(z, 2)
    stays = dest_inner == inner

    barrier = pltpu.get_barrier_semaphore()
    for d in range(1, GROUP):
        for s in pieces:
            pl.semaphore_signal(barrier, inc=1, device_id=peer(s, d), device_id_type=MESH)
    for e in range(1, 8):
        pl.semaphore_signal(barrier, inc=1, device_id=(beside[e], outer), device_id_type=MESH)
    pl.semaphore_signal(barrier, inc=1, device_id=(inner, further), device_id_type=MESH)

    @pl.when(border)
    def _():
        for i in across:
            pl.semaphore_signal(barrier, inc=1, device_id=(i, facing), device_id_type=MESH)

    for kx in range(2):
        for ky in range(4):
            for kz in range(4):
                src = (src_z[kz][0] + src_x[kx], src_y[ky] + src_z[kz][1])

                @pl.when((src[0] != inner) | (src[1] != outer))
                def _():
                    pl.semaphore_signal(barrier, inc=1, device_id=src, device_id_type=MESH)

    pl.semaphore_wait(barrier, (GROUP - 1) * PIECES + 8 + CUBES + 8 * border.astype(jnp.int32) - stays.astype(jnp.int32))

    def remote(src, dst, send, recv, dev):
        return pltpu.make_async_remote_copy(
            src_ref=src, dst_ref=dst, send_sem=send, recv_sem=recv, device_id=dev, device_id_type=MESH)

    def arrived(ref, sem):
        pltpu.make_async_copy(ref, ref, sem).wait()

    def columns(at, width):
        return pl.ds(pl.multiple_of(at, width), width)

    row_slot = pl.ds(pl.multiple_of(inner * 16, 16), 16)

    others = pl.ds(1, GROUP - 1)
    near_rows, far_rows = (pl.ds(pl.multiple_of(h, 128), 128) for h in (zh * 128, 128 - zh * 128))

    def chip(t):
        e = rem(t * 3, CHIPS)
        return e, div(e, 4), rem(div(e, 2), 2), rem(e, 2)

    def pick(pair, bit):
        return pair[0] + bit * (pair[1] - pair[0])

    def member(s, t, dc):
        e, dx, dy, dz = chip(t)
        return pick(z8[s], dz) + pick(x2[s], dx) + cs[dc], pick(y4[s], dy) + pick(zr[s], dz)

    def member_block(t, dc):
        e, dx, dy, dz = chip(t)
        return pick(bx, dx) + pick(by, dy) + pick(bz, dz) + cs[dc]

    def send_tokens(t):
        e = chip(t)[0]
        for dc in range(2):
            at = member_block(t, dc) * BLOCK
            for s in pieces:
                for a in range(2):
                    remote((acts, cot)[a].at[:, columns(at + s * W, W)], tok.at[a, s, 2 * e + dc],
                           tok_s.at[a], tok_r.at[a, s, 2 * e + dc], member(s, t, dc)).start()

    def near_tokens(a):
        for s in pieces:
            remote((acts, cot)[a].at[:, columns(block(1) * BLOCK + s * W, W)], tok.at[a, s, 1],
                   tok_s.at[a], tok_r.at[a, s, 1], peer(s, 1)).start()
            pltpu.make_async_copy((acts, cot)[a].at[:, columns(block(0) * BLOCK + s * W, W)],
                                  tok.at[a, s, 0], tok_r.at[a, s, 0]).start()

    for a in (1, 0):
        @pl.when(border)
        def _():
            for n, i in enumerate(across):
                remote((enc, dec)[a].at[:, columns((n % 4 + by[0] + bz[1]) * BLOCK, BLOCK)], rows.at[a, row_slot, :],
                       cross_s.at[a], cross_r.at[a], (i, facing)).start()

        for e in range(1, 8):
            remote((enc, dec)[a].at[:, columns((rem(beside[e], 4) + byz[0][0]) * BLOCK, BLOCK)],
                   rows.at[a, row_slot, :], row_s.at[a], row_r.at[a], (beside[e], outer)).start()
        pltpu.make_async_copy(
            (enc, dec)[a].at[:, columns(block(0) * BLOCK, BLOCK)], rows.at[a, row_slot, :], row_r.at[a]).start()
    for d in PEERS:
        for s in pieces:
            remote(ids, idsb.at[s, d], ids_s, ids_r, peer(s, d)).start()
    for s in pieces:
        idsb[s, 0] = ids[...]
    for a in range(2):
        near_tokens(a)

    @pl.loop(1, WINDOW)
    def _(t):
        send_tokens(t)

    @pl.when(border)
    def _():
        for a in (1, 0):
            arrived(rows.at[a, far_rows, :], cross_r.at[a])
            remote(rows.at[a, far_rows, :], rows.at[a, far_rows, :], relay_s.at[a], cross_r.at[a],
                   (inner, further)).start()

    latent = lax.broadcasted_iota(jnp.int32, (LB, 2 * TOK), 0)
    def both(ref):
        return jnp.concatenate([ref[0], ref[1]], axis=1)

    def partials(t):
        e = chip(t)[0]
        d = 2 * e
        for s in pieces:
            for dc in range(2):
                for a in range(2):
                    arrived(tok.at[a, s, d + dc], tok_r.at[a, s, d + dc])
        @pl.when(t < CHIPS - WINDOW)
        def _():
            send_tokens(t + WINDOW)

        for s in pieces:
            which = both(idsb[s, pl.ds(d, 2)])
            hits = [which[k:k + 1, :] == latent for k in range(K)]
            out = []
            for a in range(2):
                full = lax.dot_general(rows[a, :, s * W:(s + 1) * W], tok[a, s, pl.ds(d, 2)].reshape(2 * TOK, W),
                                       (((1,), (1,)), ((), ())), preferred_element_type=jnp.float32)
                for k in range(K):
                    out.append(jnp.sum(jnp.where(hits[k], full, 0.0), axis=0, keepdims=True))
            out = jnp.concatenate(out, axis=0)
            pout[s, d] = out[:, :TOK]
            pout[s, d + 1] = out[:, TOK:]

        def send(s, dc):
            remote(pout.at[s, d + dc], pin.at[s, d + dc], p_s, p_r, member(s, t, dc)).start()

        @pl.when(t == 0)
        def _():
            for s in pieces:
                pin[s, 0] = pout[s, 0]

        @pl.when(t > 0)
        def _():
            for s in pieces:
                send(s, 0)
        for s in pieces:
            send(s, 1)

    def send_codes():
        arrived(pin.at[:, others], p_r)
        codes = jnp.sum(pin[...].reshape(PIECES * GROUP, 2 * K, TOK), axis=0)
        cout[...] = codes.astype(jnp.bfloat16).astype(jnp.float32)
        for d in PEERS:
            for s in pieces:
                remote(cout, cin.at[s, d], c_s, c_r, peer(s, d)).start()
        for s in pieces:
            cin[s, 0] = cout[...]

    def spread_codes(s):
        @pl.loop(0, CHIPS)
        def _(e):
            which, values = both(idsb[s, pl.ds(2 * e, 2)]), both(cin[s, pl.ds(2 * e, 2)])
            hits = [which[k:k + 1, :] == latent for k in range(K)]
            at = pl.ds(pl.multiple_of(e * 2 * TOK, 2 * TOK), 2 * TOK)
            for a in range(2):
                full = jnp.zeros((LB, 2 * TOK), jnp.float32)
                for k in range(K):
                    full = jnp.where(hits[k], values[a * K + k:a * K + k + 1, :], full)
                spread[a, s, :, at] = full.astype(jnp.bfloat16)

    def term(s):
        out = [lax.dot_general(spread[1 - a, s], tok[a, s].reshape(GROUP * TOK, W), (((1,), (0,)), ((), ())),
                               preferred_element_type=jnp.float32).reshape(CUBES, 8, W) for a in range(2)]
        tsend[s] = jnp.concatenate(out, axis=1).astype(jnp.bfloat16)

    def send_term(s):
        @pl.when(stays)
        def _():
            pltpu.make_async_copy(tsend.at[s, outer], fin.at[s, cube], f_r.at[s]).start()

        @pl.when(jnp.logical_not(stays))
        def _():
            remote(tsend.at[s, outer], fin.at[s, cube], f_s.at[s], f_r.at[s], (dest_inner, outer)).start()

        for at in dests[1:]:
            remote(tsend.at[s, at], fin.at[s, cube], f_s.at[s], f_r.at[s], (dest_inner, at)).start()

    def total(s):
        arrived(fin.at[s], f_r.at[s])
        both_grads = jnp.sum(fin[s].astype(jnp.float32), axis=0)
        oenc[:, s * W:(s + 1) * W] = both_grads[:8]
        odec[:, s * W:(s + 1) * W] = both_grads[8:]

    for a in (1, 0):
        arrived(rows.at[a, near_rows, :], row_r.at[a])

        @pl.when(jnp.logical_not(border))
        def _():
            arrived(rows.at[a, far_rows, :], cross_r.at[a])
    arrived(idsb.at[:, others], ids_r)

    @pl.loop(0, CHIPS)
    def _(t):
        partials(t)

    for a in range(2):
        arrived(rows.at[a, pl.ds(0, LB // 2 - 16), :], row_s.at[a])

        @pl.when(border)
        def _():
            arrived(rows.at[a, far_rows, :], cross_s.at[a])
            arrived(rows.at[a, far_rows, :], relay_s.at[a])
        arrived(tok.at[a, :, others], tok_s.at[a])
    arrived(idsb.at[:, others], ids_s)

    send_codes()
    arrived(pout.at[:, others], p_s)
    arrived(cin.at[:, others], c_r)
    for s in pieces:
        spread_codes(s)
        term(s)
        send_term(s)
    arrived(cin.at[:, others], c_s)
    for s in pieces:
        total(s)
    for s in pieces:
        @pl.when(stays)
        def _():
            arrived(tsend.at[s, pl.ds(1, CUBES - 1)], f_s.at[s])

        @pl.when(jnp.logical_not(stays))
        def _():
            arrived(tsend.at[s], f_s.at[s])


def local(acts, cotangent, latent_ids, enc_rows, dec_rows):
    S, W = PIECES, BLOCK // PIECES
    ids = latent_ids.T
    ids = jnp.concatenate([ids, ids], axis=0)
    vmem, hbm = pl.BlockSpec(memory_space=pltpu.VMEM), pl.BlockSpec(memory_space=pl.ANY)
    dma = pltpu.SemaphoreType.DMA
    two = dma((2,))
    return pl.pallas_call(
        kernel,
        out_shape=(jax.ShapeDtypeStruct((8, BLOCK), jnp.float32),) * 2,
        in_specs=[hbm, hbm, vmem, hbm, hbm],
        out_specs=(vmem, vmem),
        scratch_shapes=[
            pltpu.VMEM((2, S, GROUP, TOK, W), jnp.bfloat16),
            pltpu.VMEM((2, LB, BLOCK), jnp.bfloat16),
            pltpu.VMEM((S, GROUP, 8, TOK), jnp.int32),
            pltpu.VMEM((S, GROUP, 8, TOK), jnp.float32),
            pltpu.VMEM((S, GROUP, 8, TOK), jnp.float32),
            pltpu.VMEM((8, TOK), jnp.float32),
            pltpu.VMEM((S, GROUP, 8, TOK), jnp.float32),
            pltpu.VMEM((2, S, LB, GROUP * TOK), jnp.bfloat16),
            pltpu.VMEM((S, CUBES, 16, W), jnp.bfloat16),
            pltpu.VMEM((S, CUBES, 16, W), jnp.bfloat16),
            two, dma((2, S, GROUP)),
            two, two, two, two, two,
            dma, dma, dma, dma, dma, dma, dma((S,)), dma((S,)),
        ],
        compiler_params=pltpu.CompilerParams(
            collective_id=0, has_side_effects=True, vmem_limit_bytes=60 * 2**20),
    )(acts, cotangent, ids, enc_rows, dec_rows)


def solution(mesh):
    placed = (
        P(("inner", "outer"), None),
        P(("inner", "outer"), None),
        P(("inner", "outer"), None),
        P("inner", None),
        P("inner", None),
    )
    return jax.shard_map(
        local,
        mesh=mesh,
        in_specs=placed,
        out_specs=(P("outer", "inner"), P("outer", "inner")),
        check_vma=False,
    )
```

```python
import functools

import jax
import jax.numpy as jnp
from jax import lax
from jax.experimental import pallas as pl
from jax.experimental.pallas import tpu as pltpu
from jax.sharding import PartitionSpec as P

MESH = pl.DeviceIdType.MESH
NX, NY, NZ = 4, 8, 8
TOK, LB, BLOCK = 128, 256, 512
HALF = BLOCK // 2
K = 4
SHIFTS = ((0, 0, 0), (1, 0, 0), (-1, 0, 0), (0, 1, 0), (0, -1, 0), (0, 0, 1), (0, 0, -1), (0, 1, 1), (0, -1, -1))
OPPOSITE = (0, 2, 1, 4, 3, 6, 5, 8, 7)
CHIPS = 9
WHOLE = 7
SOURCES = 32


def div(a, b):
    return lax.div(a, jnp.int32(b))


def rem(a, b):
    return lax.rem(a, jnp.int32(b))


def kernel(acts, cot, ids, enc, dec, oenc, odec,
           tok, tokh, rows, idsb, pout, pin, cout, cin, spread, tsend, fin,
           tok_s, tok_r, half_s, half_r, row_s, row_r, cross_s, cross_r, relay_s,
           ids_s, ids_r, p_s, p_r, c_s, c_r, f_s, f_r):
    inner, outer = lax.axis_index("inner"), lax.axis_index("outer")
    zh, x, c = div(inner, 8), rem(div(inner, 2), 4), rem(inner, 2)
    y, zl = div(outer, 4), rem(outer, 4)
    z = zh * 4 + zl
    number = rem(2 * x + y + 3 * z, 8)
    halves = range(2)

    cs = (c, 1 - c)
    xs = {d: rem(x + NX + d, NX) * 2 for d in (-1, 0, 1)}
    ys = {d: rem(y + NY + d, NY) * 4 for d in (-1, 0, 1)}
    zs = {d: rem(z + NZ + d, NZ) for d in (-1, 0, 1)}
    zs = {d: (div(v, 4) * 8, rem(v, 4)) for d, v in zs.items()}

    def member(j, dc):
        dx, dy, dz = SHIFTS[j]
        return zs[dz][0] + xs[dx] + cs[dc], ys[dy] + zs[dz][1]

    def owner(j, dc):
        return member(OPPOSITE[j], dc)

    shift_number = [(2 * dx + dy + 3 * dz) % 8 for dx, dy, dz in SHIFTS]
    owner_number = [rem(number + (8 - n), 8) * 2 for n in shift_number]

    half = zh * 8
    beside = [rem(inner + e, 8) for e in range(8)]
    border = (zl == 0) | (zl == 3)
    facing = y * 4 + 3 - zl
    facing_number = rem(y + 3 * (7 - z), 8)
    further_x = rem(x + NX + jnp.where(zl < 2, 1, -1), NX)
    further = (half + further_x * 2 + c, y * 4 + rem(zl + 2, 4))

    wanted = zh * 4 + x
    dest_inner = number * 2 + c
    dest_y = [rem(y + dy, NY) * 4 for dy in range(NY)]
    dest_z = [rem(zl + dz, 4) for dz in range(4)]
    dests = [dest_y[dy] + dest_z[dz] for dy in range(NY) for dz in range(4)]
    source = x * 8 + z
    stays = dest_inner == inner

    barrier = pltpu.get_barrier_semaphore()
    for j in range(CHIPS):
        for dc in range(2):
            if j or dc:
                pl.semaphore_signal(barrier, inc=1, device_id=member(j, dc), device_id_type=MESH)
    for e in range(1, 8):
        pl.semaphore_signal(barrier, inc=1, device_id=(half + beside[e], outer), device_id_type=MESH)
    pl.semaphore_signal(barrier, inc=1, device_id=further, device_id_type=MESH)

    @pl.when(border)
    def _():
        for i in range(8):
            pl.semaphore_signal(barrier, inc=1, device_id=(8 - half + i, facing), device_id_type=MESH)

    for z1 in range(NZ):
        for x1 in range(NX):
            y1 = rem(wanted + (64 - 2 * x1 - 3 * z1), 8)
            src = ((z1 // 4) * 8 + x1 * 2 + c, y1 * 4 + z1 % 4)

            @pl.when((src[0] != inner) | (src[1] != outer))
            def _():
                pl.semaphore_signal(barrier, inc=1, device_id=src, device_id_type=MESH)

    pl.semaphore_wait(barrier, 2 * CHIPS - 1 + 8 + SOURCES + 8 * border.astype(jnp.int32) - stays.astype(jnp.int32))

    def remote(src, dst, send, recv, dev):
        return pltpu.make_async_remote_copy(
            src_ref=src, dst_ref=dst, send_sem=send, recv_sem=recv, device_id=dev, device_id_type=MESH)

    def arrived(ref, sem):
        pltpu.make_async_copy(ref, ref, sem).wait()

    def columns(at, width):
        return pl.ds(pl.multiple_of(at, width), width)

    row_slot = pl.ds(pl.multiple_of(inner * 16, 16), 16)
    others = pl.ds(1, 2 * CHIPS - 1)
    near_rows, far_rows = (pl.ds(pl.multiple_of(h, 128), 128) for h in (zh * 128, 128 - zh * 128))

    for a in range(2):
        @pl.when(border)
        def _():
            for i in range(8):
                at = rem(facing_number + 2 * (i // 2), 8) * 2 + i % 2
                remote((enc, dec)[a].at[:, columns(at * BLOCK, BLOCK)], rows.at[a, row_slot, :],
                       cross_s.at[a], cross_r.at[a], (8 - half + i, facing)).start()

        for e in range(1, 8):
            at = rem(2 * div(beside[e], 2) + y + 3 * z, 8) * 2 + rem(beside[e], 2)
            remote((enc, dec)[a].at[:, columns(at * BLOCK, BLOCK)],
                   rows.at[a, row_slot, :], row_s.at[a], row_r.at[a], (half + beside[e], outer)).start()
        pltpu.make_async_copy(
            (enc, dec)[a].at[:, columns(dest_inner * BLOCK, BLOCK)], rows.at[a, row_slot, :], row_r.at[a]).start()
    for j in range(CHIPS):
        for dc in range(2):
            if j or dc:
                remote(ids, idsb.at[2 * j + dc], ids_s, ids_r, owner(j, dc)).start()
    idsb[0] = ids[...]
    for j in (7, 8, 0, 1, 2, 3, 4, 5, 6):
        for dc in range(2):
            at = (owner_number[j] + cs[dc]) * BLOCK
            for a in range(2):
                if j >= WHOLE:
                    h = j - WHOLE
                    remote((acts, cot)[a].at[:, columns(at + h * HALF, HALF)], tokh.at[a, h, dc],
                           half_s.at[a], half_r.at[a, h, dc], owner(j, dc)).start()
                elif j or dc:
                    remote((acts, cot)[a].at[:, columns(at, BLOCK)], tok.at[a, 2 * j + dc],
                           tok_s.at[a], tok_r.at[a, 2 * j + dc], owner(j, dc)).start()
                else:
                    pltpu.make_async_copy((acts, cot)[a].at[:, columns(at, BLOCK)], tok.at[a, 0], tok_r.at[a, 0]).start()

    @pl.when(border)
    def _():
        for a in range(2):
            arrived(rows.at[a, far_rows, :], cross_r.at[a])
            remote(rows.at[a, far_rows, :], rows.at[a, far_rows, :], relay_s.at[a], cross_r.at[a], further).start()

    latent = lax.broadcasted_iota(jnp.int32, (LB, 2 * TOK), 0)

    def both(ref):
        return jnp.concatenate([ref[0], ref[1]], axis=1)

    def partials(j, left, right):
        which = both(idsb[pl.ds(2 * j, 2)])
        hits = [which[k:k + 1, :] == latent for k in range(K)]
        out = []
        for a in range(2):
            full = lax.dot_general(left(a), right(a), (((1,), (1,)), ((), ())), preferred_element_type=jnp.float32)
            for k in range(K):
                out.append(jnp.sum(jnp.where(hits[k], full, 0.0), axis=0, keepdims=True))
        out = jnp.concatenate(out, axis=0)
        pout[2 * j] = out[:, :TOK]
        pout[2 * j + 1] = out[:, TOK:]

    def send_partials(j):
        for dc in range(2):
            if j or dc:
                remote(pout.at[2 * j + dc], pin.at[2 * j + dc], p_s, p_r, member(j, dc)).start()
            else:
                pin[0] = pout[0]

    for a in range(2):
        arrived(rows.at[a, near_rows, :], row_r.at[a])

        @pl.when(jnp.logical_not(border))
        def _():
            arrived(rows.at[a, far_rows, :], cross_r.at[a])
    arrived(idsb.at[others], ids_r)

    @pl.loop(0, WHOLE)
    def _(j):
        for a in range(2):
            for dc in range(2):
                arrived(tok.at[a, 2 * j + dc], tok_r.at[a, 2 * j + dc])
        partials(j, lambda a: rows[a], lambda a: tok[a, pl.ds(2 * j, 2)].reshape(2 * TOK, BLOCK))
        for at in range(WHOLE):
            @pl.when(j == at)
            def _():
                send_partials(at)

    for h in halves:
        for a in range(2):
            for dc in range(2):
                arrived(tokh.at[a, h, dc], half_r.at[a, h, dc])
        partials(WHOLE + h, lambda a: rows[a, :, h * HALF:(h + 1) * HALF], lambda a: tokh[a, h].reshape(2 * TOK, HALF))
        send_partials(WHOLE + h)

    for a in range(2):
        arrived(rows.at[a, pl.ds(0, LB // 2 - 16), :], row_s.at[a])

        @pl.when(border)
        def _():
            arrived(rows.at[a, far_rows, :], cross_s.at[a])
            arrived(rows.at[a, far_rows, :], relay_s.at[a])
        arrived(tok.at[a, pl.ds(1, 2 * WHOLE - 1)], tok_s.at[a])
        arrived(tokh.at[a], half_s.at[a])
    arrived(idsb.at[others], ids_s)

    arrived(pin.at[others], p_r)
    codes = jnp.sum(pin[...], axis=0)
    cout[...] = codes.astype(jnp.bfloat16).astype(jnp.float32)
    for j in range(CHIPS):
        for dc in range(2):
            if j or dc:
                remote(cout, cin.at[2 * j + dc], c_s, c_r, owner(j, dc)).start()
    cin[0] = cout[...]
    arrived(pout.at[others], p_s)
    arrived(cin.at[others], c_r)

    @pl.loop(0, CHIPS)
    def _(j):
        which, values = both(idsb[pl.ds(2 * j, 2)]), both(cin[pl.ds(2 * j, 2)])
        hits = [which[k:k + 1, :] == latent for k in range(K)]
        at = columns(j * 2 * TOK, 2 * TOK)
        for a in range(2):
            full = jnp.zeros((LB, 2 * TOK), jnp.float32)
            for k in range(K):
                full = jnp.where(hits[k], values[a * K + k:a * K + k + 1, :], full)
            spread[a, :, at] = full.astype(jnp.bfloat16)

    split = 2 * WHOLE * TOK

    def term(a, h):
        def product(left, right):
            return lax.dot_general(left, right, (((1,), (0,)), ((), ())), preferred_element_type=jnp.float32)

        at = split + h * 2 * TOK
        out = product(spread[1 - a, :, :split], tok[a, :, :, h * HALF:(h + 1) * HALF].reshape(split, HALF))
        out = out + product(spread[1 - a, :, at:at + 2 * TOK], tokh[a, h].reshape(2 * TOK, HALF))
        return out.reshape(SOURCES, 8, HALF)

    for h in halves:
        tsend[h] = jnp.concatenate([term(a, h) for a in range(2)], axis=1).astype(jnp.bfloat16)

        @pl.when(stays)
        def _():
            pltpu.make_async_copy(tsend.at[h, outer], fin.at[h, source], f_r.at[h]).start()

        @pl.when(jnp.logical_not(stays))
        def _():
            remote(tsend.at[h, outer], fin.at[h, source], f_s.at[h], f_r.at[h], (dest_inner, outer)).start()

        for at in dests[1:]:
            remote(tsend.at[h, at], fin.at[h, source], f_s.at[h], f_r.at[h], (dest_inner, at)).start()

    arrived(cin.at[others], c_s)
    for h in halves:
        arrived(fin.at[h], f_r.at[h])
        both_grads = jnp.sum(fin[h].astype(jnp.float32), axis=0)
        oenc[:, h * HALF:(h + 1) * HALF] = both_grads[:8]
        odec[:, h * HALF:(h + 1) * HALF] = both_grads[8:]
    for h in halves:
        @pl.when(stays)
        def _():
            arrived(tsend.at[h, pl.ds(1, SOURCES - 1)], f_s.at[h])

        @pl.when(jnp.logical_not(stays))
        def _():
            arrived(tsend.at[h], f_s.at[h])


def local(acts, cotangent, latent_ids, enc_rows, dec_rows):
    ids = latent_ids.T
    ids = jnp.concatenate([ids, ids], axis=0)
    vmem, hbm = pl.BlockSpec(memory_space=pltpu.VMEM), pl.BlockSpec(memory_space=pl.ANY)
    dma = pltpu.SemaphoreType.DMA
    two = dma((2,))
    return pl.pallas_call(
        kernel,
        out_shape=(jax.ShapeDtypeStruct((8, BLOCK), jnp.float32),) * 2,
        in_specs=[hbm, hbm, vmem, hbm, hbm],
        out_specs=(vmem, vmem),
        scratch_shapes=[
            pltpu.VMEM((2, 2 * WHOLE, TOK, BLOCK), jnp.bfloat16),
            pltpu.VMEM((2, 2, 2, TOK, HALF), jnp.bfloat16),
            pltpu.VMEM((2, LB, BLOCK), jnp.bfloat16),
            pltpu.VMEM((2 * CHIPS, 8, TOK), jnp.int32),
            pltpu.VMEM((2 * CHIPS, 8, TOK), jnp.float32),
            pltpu.VMEM((2 * CHIPS, 8, TOK), jnp.float32),
            pltpu.VMEM((8, TOK), jnp.float32),
            pltpu.VMEM((2 * CHIPS, 8, TOK), jnp.float32),
            pltpu.VMEM((2, LB, 2 * CHIPS * TOK), jnp.bfloat16),
            pltpu.VMEM((2, SOURCES, 16, HALF), jnp.bfloat16),
            pltpu.VMEM((2, SOURCES, 16, HALF), jnp.bfloat16),
            two, dma((2, 2 * WHOLE)), two, dma((2, 2, 2)),
            two, two, two, two, two,
            dma, dma, dma, dma, dma, dma, two, two,
        ],
        compiler_params=pltpu.CompilerParams(
            collective_id=0, has_side_effects=True, vmem_limit_bytes=60 * 2**20),
    )(acts, cotangent, ids, enc_rows, dec_rows)


def solution(mesh):
    placed = (
        P(("inner", "outer"), None),
        P(("inner", "outer"), None),
        P(("inner", "outer"), None),
        P("inner", None),
        P("inner", None),
    )
    return jax.shard_map(
        local,
        mesh=mesh,
        in_specs=placed,
        out_specs=(P("outer", "inner"), P("outer", "inner")),
        check_vma=False,
    )
```

```python
import functools

import jax
import jax.numpy as jnp
from jax import lax
from jax.experimental import pallas as pl
from jax.experimental.pallas import tpu as pltpu
from jax.sharding import PartitionSpec as P

MESH = pl.DeviceIdType.MESH
NX, NY, NZ = 4, 8, 8
TOK, LB, BLOCK = 128, 256, 512
HALF = BLOCK // 2
K = 4
SHIFTS = ((0, 0, 0), (1, 0, 0), (-1, 0, 0), (0, 1, 0), (0, -1, 0), (0, 0, 1), (0, 0, -1), (0, 1, 1), (0, -1, -1))
OPPOSITE = (0, 2, 1, 4, 3, 6, 5, 8, 7)
CHIPS = 9
WHOLE = 7
SOURCES = 32


def div(a, b):
    return lax.div(a, jnp.int32(b))


def rem(a, b):
    return lax.rem(a, jnp.int32(b))


def kernel(acts, cot, ids, enc, dec, oenc, odec,
           tok, tokh, rows, idsb, pout, pin, cout, cin, spread, tsend, fin,
           tok_s, tok_r, half_s, half_r, row_s, row_r, cross_s, cross_r, relay_s,
           ids_s, ids_r, p_s, p_r, c_s, c_r, f_s, f_r):
    inner, outer = lax.axis_index("inner"), lax.axis_index("outer")
    zh, x, c = div(inner, 8), rem(div(inner, 2), 4), rem(inner, 2)
    y, zl = div(outer, 4), rem(outer, 4)
    z = zh * 4 + zl
    number = rem(2 * x + y + 3 * z, 8)
    halves = range(2)

    cs = (c, 1 - c)
    xs = {d: rem(x + NX + d, NX) * 2 for d in (-1, 0, 1)}
    ys = {d: rem(y + NY + d, NY) * 4 for d in (-1, 0, 1)}
    zs = {d: rem(z + NZ + d, NZ) for d in (-1, 0, 1)}
    zs = {d: (div(v, 4) * 8, rem(v, 4)) for d, v in zs.items()}

    def member(j, dc):
        dx, dy, dz = SHIFTS[j]
        return zs[dz][0] + xs[dx] + cs[dc], ys[dy] + zs[dz][1]

    def owner(j, dc):
        return member(OPPOSITE[j], dc)

    shift_number = [(2 * dx + dy + 3 * dz) % 8 for dx, dy, dz in SHIFTS]
    owner_number = [rem(number + (8 - n), 8) * 2 for n in shift_number]

    half = zh * 8
    beside = [rem(inner + e, 8) for e in range(8)]
    border = (zl == 0) | (zl == 3)
    facing = y * 4 + 3 - zl
    facing_number = rem(y + 3 * (7 - z), 8)
    further_x = rem(x + NX + jnp.where(zl < 2, 1, -1), NX)
    further = (half + further_x * 2 + c, y * 4 + rem(zl + 2, 4))

    wanted = zh * 4 + x
    dest_inner = number * 2 + c
    dest_y = [rem(y + dy, NY) * 4 for dy in range(NY)]
    dest_z = [rem(zl + dz, 4) for dz in range(4)]
    dests = [dest_y[dy] + dest_z[dz] for dy in range(NY) for dz in range(4)]
    source = x * 8 + z
    stays = dest_inner == inner

    def columns(at, width):
        return pl.ds(pl.multiple_of(at, width), width)

    row_slot = pl.ds(pl.multiple_of(inner * 16, 16), 16)

    for a in range(2):
        pltpu.make_async_copy(
            (enc, dec)[a].at[:, columns(dest_inner * BLOCK, BLOCK)], rows.at[a, row_slot, :], row_r.at[a]).start()
        pltpu.make_async_copy(
            (acts, cot)[a].at[:, columns(dest_inner * BLOCK, BLOCK)], tok.at[a, 0], tok_r.at[a, 0]).start()
    idsb[0] = ids[...]

    barrier = pltpu.get_barrier_semaphore()
    for j in range(CHIPS):
        for dc in range(2):
            if j or dc:
                pl.semaphore_signal(barrier, inc=1, device_id=member(j, dc), device_id_type=MESH)
    for e in range(1, 8):
        pl.semaphore_signal(barrier, inc=1, device_id=(half + beside[e], outer), device_id_type=MESH)
    pl.semaphore_signal(barrier, inc=1, device_id=further, device_id_type=MESH)

    @pl.when(border)
    def _():
        for i in range(8):
            pl.semaphore_signal(barrier, inc=1, device_id=(8 - half + i, facing), device_id_type=MESH)

    for z1 in range(NZ):
        for x1 in range(NX):
            y1 = rem(wanted + (64 - 2 * x1 - 3 * z1), 8)
            src = ((z1 // 4) * 8 + x1 * 2 + c, y1 * 4 + z1 % 4)

            @pl.when((src[0] != inner) | (src[1] != outer))
            def _():
                pl.semaphore_signal(barrier, inc=1, device_id=src, device_id_type=MESH)

    pl.semaphore_wait(barrier, 2 * CHIPS - 1 + 8 + SOURCES + 8 * border.astype(jnp.int32) - stays.astype(jnp.int32))

    def remote(src, dst, send, recv, dev):
        return pltpu.make_async_remote_copy(
            src_ref=src, dst_ref=dst, send_sem=send, recv_sem=recv, device_id=dev, device_id_type=MESH)

    def arrived(ref, sem):
        pltpu.make_async_copy(ref, ref, sem).wait()

    others = pl.ds(1, 2 * CHIPS - 1)
    near_rows, far_rows = (pl.ds(pl.multiple_of(h, 128), 128) for h in (zh * 128, 128 - zh * 128))

    for a in range(2):
        @pl.when(border)
        def _():
            for i in range(8):
                at = rem(facing_number + 2 * (i // 2), 8) * 2 + i % 2
                remote((enc, dec)[a].at[:, columns(at * BLOCK, BLOCK)], rows.at[a, row_slot, :],
                       cross_s.at[a], cross_r.at[a], (8 - half + i, facing)).start()

        for e in range(1, 8):
            at = rem(2 * div(beside[e], 2) + y + 3 * z, 8) * 2 + rem(beside[e], 2)
            remote((enc, dec)[a].at[:, columns(at * BLOCK, BLOCK)],
                   rows.at[a, row_slot, :], row_s.at[a], row_r.at[a], (half + beside[e], outer)).start()
    for j in range(CHIPS):
        for dc in range(2):
            if j or dc:
                remote(ids, idsb.at[2 * j + dc], ids_s, ids_r, owner(j, dc)).start()
    for j in (7, 8, 0, 1, 2, 3, 4, 5, 6):
        for dc in range(2):
            at = (owner_number[j] + cs[dc]) * BLOCK
            for a in range(2):
                if j >= WHOLE:
                    h = j - WHOLE
                    remote((acts, cot)[a].at[:, columns(at + h * HALF, HALF)], tokh.at[a, h, dc],
                           half_s.at[a], half_r.at[a, h, dc], owner(j, dc)).start()
                elif j or dc:
                    remote((acts, cot)[a].at[:, columns(at, BLOCK)], tok.at[a, 2 * j + dc],
                           tok_s.at[a], tok_r.at[a, 2 * j + dc], owner(j, dc)).start()

    @pl.when(border)
    def _():
        for a in range(2):
            arrived(rows.at[a, far_rows, :], cross_r.at[a])
            remote(rows.at[a, far_rows, :], rows.at[a, far_rows, :], relay_s.at[a], cross_r.at[a], further).start()

    latent = lax.broadcasted_iota(jnp.int32, (LB, 2 * TOK), 0)

    def both(ref):
        return jnp.concatenate([ref[0], ref[1]], axis=1)

    def partials(j, left, right):
        which = both(idsb[pl.ds(2 * j, 2)])
        hits = [which[k:k + 1, :] == latent for k in range(K)]
        out = []
        for a in range(2):
            full = lax.dot_general(left(a), right(a), (((1,), (1,)), ((), ())), preferred_element_type=jnp.float32)
            for k in range(K):
                out.append(jnp.sum(jnp.where(hits[k], full, 0.0), axis=0, keepdims=True))
        out = jnp.concatenate(out, axis=0)
        pout[2 * j] = out[:, :TOK]
        pout[2 * j + 1] = out[:, TOK:]

    def send_partials(j):
        for dc in range(2):
            if j or dc:
                remote(pout.at[2 * j + dc], pin.at[2 * j + dc], p_s, p_r, member(j, dc)).start()
            else:
                pin[0] = pout[0]

    for a in range(2):
        arrived(rows.at[a, near_rows, :], row_r.at[a])

        @pl.when(jnp.logical_not(border))
        def _():
            arrived(rows.at[a, far_rows, :], cross_r.at[a])
    arrived(idsb.at[others], ids_r)

    def left(j):
        h = j - WHOLE
        return lambda a: rows[a] if j < WHOLE else rows[a, :, h * HALF:(h + 1) * HALF]

    def right(j):
        return lambda a: (tok[a, 2 * j:2 * j + 2].reshape(2 * TOK, BLOCK) if j < WHOLE else
                          tokh[a, j - WHOLE].reshape(2 * TOK, HALF))

    for group in ((0, 1, 2), (3, 4, 5), (6, 7, 8)):
        for j in group:
            for a in range(2):
                for dc in range(2):
                    if j < WHOLE:
                        arrived(tok.at[a, 2 * j + dc], tok_r.at[a, 2 * j + dc])
                    else:
                        arrived(tokh.at[a, j - WHOLE, dc], half_r.at[a, j - WHOLE, dc])
        for j in group:
            partials(j, left(j), right(j))
        for j in group:
            send_partials(j)

    for a in range(2):
        arrived(rows.at[a, pl.ds(0, LB // 2 - 16), :], row_s.at[a])

        @pl.when(border)
        def _():
            arrived(rows.at[a, far_rows, :], cross_s.at[a])
            arrived(rows.at[a, far_rows, :], relay_s.at[a])
        arrived(tok.at[a, pl.ds(1, 2 * WHOLE - 1)], tok_s.at[a])
        arrived(tokh.at[a], half_s.at[a])
    arrived(idsb.at[others], ids_s)

    arrived(pin.at[others], p_r)
    codes = jnp.sum(pin[...], axis=0)
    cout[...] = codes.astype(jnp.bfloat16).astype(jnp.float32)
    for j in range(CHIPS):
        for dc in range(2):
            if j or dc:
                remote(cout, cin.at[2 * j + dc], c_s, c_r, owner(j, dc)).start()
    cin[0] = cout[...]
    arrived(pout.at[others], p_s)
    arrived(cin.at[others], c_r)

    latent16 = latent.astype(jnp.float32).astype(jnp.bfloat16)

    @pl.loop(0, CHIPS)
    def _(j):
        which = both(idsb[pl.ds(2 * j, 2)]).astype(jnp.float32).astype(jnp.bfloat16)
        values = both(cin[pl.ds(2 * j, 2)]).astype(jnp.bfloat16)
        hits = [which[k:k + 1, :] == latent16 for k in range(K)]
        at = columns(j * 2 * TOK, 2 * TOK)
        for a in range(2):
            full = jnp.zeros((LB, 2 * TOK), jnp.bfloat16)
            for k in range(K):
                full = jnp.where(hits[k], values[a * K + k:a * K + k + 1, :], full)
            spread[a, :, at] = full

    split = 2 * WHOLE * TOK

    def term(a, h):
        def product(left, right):
            return lax.dot_general(left, right, (((1,), (0,)), ((), ())), preferred_element_type=jnp.float32)

        at = split + h * 2 * TOK
        out = product(spread[1 - a, :, :split], tok[a, :, :, h * HALF:(h + 1) * HALF].reshape(split, HALF))
        out = out + product(spread[1 - a, :, at:at + 2 * TOK], tokh[a, h].reshape(2 * TOK, HALF))
        return out.reshape(SOURCES, 8, HALF)

    for h in halves:
        tsend[h] = jnp.concatenate([term(a, h) for a in range(2)], axis=1).astype(jnp.bfloat16)

        @pl.when(stays)
        def _():
            pltpu.make_async_copy(tsend.at[h, outer], fin.at[h, source], f_r.at[h]).start()

        @pl.when(jnp.logical_not(stays))
        def _():
            remote(tsend.at[h, outer], fin.at[h, source], f_s.at[h], f_r.at[h], (dest_inner, outer)).start()

        for at in dests[1:]:
            remote(tsend.at[h, at], fin.at[h, source], f_s.at[h], f_r.at[h], (dest_inner, at)).start()

    arrived(cin.at[others], c_s)
    for h in halves:
        arrived(fin.at[h], f_r.at[h])
        both_grads = jnp.sum(fin[h].astype(jnp.float32), axis=0)
        oenc[:, h * HALF:(h + 1) * HALF] = both_grads[:8]
        odec[:, h * HALF:(h + 1) * HALF] = both_grads[8:]
    for h in halves:
        @pl.when(stays)
        def _():
            arrived(tsend.at[h, pl.ds(1, SOURCES - 1)], f_s.at[h])

        @pl.when(jnp.logical_not(stays))
        def _():
            arrived(tsend.at[h], f_s.at[h])


def local(acts, cotangent, latent_ids, enc_rows, dec_rows):
    ids = latent_ids.T
    vmem, hbm = pl.BlockSpec(memory_space=pltpu.VMEM), pl.BlockSpec(memory_space=pl.ANY)
    dma = pltpu.SemaphoreType.DMA
    two = dma((2,))
    return pl.pallas_call(
        kernel,
        out_shape=(jax.ShapeDtypeStruct((8, BLOCK), jnp.float32),) * 2,
        in_specs=[hbm, hbm, vmem, hbm, hbm],
        out_specs=(vmem, vmem),
        scratch_shapes=[
            pltpu.VMEM((2, 2 * WHOLE, TOK, BLOCK), jnp.bfloat16),
            pltpu.VMEM((2, 2, 2, TOK, HALF), jnp.bfloat16),
            pltpu.VMEM((2, LB, BLOCK), jnp.bfloat16),
            pltpu.VMEM((2 * CHIPS, K, TOK), jnp.int32),
            pltpu.VMEM((2 * CHIPS, 8, TOK), jnp.float32),
            pltpu.VMEM((2 * CHIPS, 8, TOK), jnp.float32),
            pltpu.VMEM((8, TOK), jnp.float32),
            pltpu.VMEM((2 * CHIPS, 8, TOK), jnp.float32),
            pltpu.VMEM((2, LB, 2 * CHIPS * TOK), jnp.bfloat16),
            pltpu.VMEM((2, SOURCES, 16, HALF), jnp.bfloat16),
            pltpu.VMEM((2, SOURCES, 16, HALF), jnp.bfloat16),
            two, dma((2, 2 * WHOLE)), two, dma((2, 2, 2)),
            two, two, two, two, two,
            dma, dma, dma, dma, dma, dma, two, two,
        ],
        compiler_params=pltpu.CompilerParams(
            collective_id=0, has_side_effects=True, vmem_limit_bytes=60 * 2**20),
    )(acts, cotangent, ids, enc_rows, dec_rows)


def solution(mesh):
    placed = (
        P(("inner", "outer"), None),
        P(("inner", "outer"), None),
        P(("inner", "outer"), None),
        P("inner", None),
        P("inner", None),
    )
    return jax.shard_map(
        local,
        mesh=mesh,
        in_specs=placed,
        out_specs=(P("outer", "inner"), P("outer", "inner")),
        check_vma=False,
    )
```

```python
import functools

import jax
import jax.numpy as jnp
from jax import lax
from jax.experimental import pallas as pl
from jax.experimental.pallas import tpu as pltpu
from jax.sharding import PartitionSpec as P

MESH = pl.DeviceIdType.MESH
NX, NY, NZ = 4, 8, 8
TOK, LB, BLOCK = 128, 256, 512
HALF = BLOCK // 2
K = 4
SHIFTS = ((0, 0, 0), (1, 0, 0), (-1, 0, 0), (0, 1, 0), (0, -1, 0), (0, 0, 1), (0, 0, -1), (0, 1, 1), (0, -1, -1))
OPPOSITE = (0, 2, 1, 4, 3, 6, 5, 8, 7)
CHIPS = 9
WHOLE = 7
SOURCES = 32


def div(a, b):
    return lax.div(a, jnp.int32(b))


def rem(a, b):
    return lax.rem(a, jnp.int32(b))


def kernel(acts, cot, ids, enc, dec, oenc, odec,
           tok, tokh, rows, idsb, pout, pin, cout, cin, spread, tsend, fin,
           tok_s, tok_r, half_s, half_r, row_s, row_r, cross_s, cross_r, relay_s,
           ids_s, ids_r, p_s, p_r, c_s, c_r, f_s, f_r):
    inner, outer = lax.axis_index("inner"), lax.axis_index("outer")
    zh, x, c = div(inner, 8), rem(div(inner, 2), 4), rem(inner, 2)
    y, zl = div(outer, 4), rem(outer, 4)
    z = zh * 4 + zl
    number = rem(2 * x + y + 3 * z, 8)
    halves = range(2)

    cs = (c, 1 - c)
    xs = {d: rem(x + NX + d, NX) * 2 for d in (-1, 0, 1)}
    ys = {d: rem(y + NY + d, NY) * 4 for d in (-1, 0, 1)}
    zs = {d: rem(z + NZ + d, NZ) for d in (-1, 0, 1)}
    zs = {d: (div(v, 4) * 8, rem(v, 4)) for d, v in zs.items()}

    def member(j, dc):
        dx, dy, dz = SHIFTS[j]
        return zs[dz][0] + xs[dx] + cs[dc], ys[dy] + zs[dz][1]

    def owner(j, dc):
        return member(OPPOSITE[j], dc)

    shift_number = [(2 * dx + dy + 3 * dz) % 8 for dx, dy, dz in SHIFTS]
    owner_number = [rem(number + (8 - n), 8) * 2 for n in shift_number]

    half = zh * 8
    beside = [rem(inner + e, 8) for e in range(8)]
    border = (zl == 0) | (zl == 3)
    facing = y * 4 + 3 - zl
    facing_number = rem(y + 3 * (7 - z), 8)
    further_x = rem(x + NX + jnp.where(zl < 2, 1, -1), NX)
    further = (half + further_x * 2 + c, y * 4 + rem(zl + 2, 4))

    wanted = zh * 4 + x
    dest_inner = number * 2 + c
    dest_y = [rem(y + dy, NY) * 4 for dy in range(NY)]
    dest_z = [rem(zl + dz, 4) for dz in range(4)]
    dests = [dest_y[dy] + dest_z[dz] for dy in range(NY) for dz in range(4)]
    source = x * 8 + z
    stays = dest_inner == inner

    def columns(at, width):
        return pl.ds(pl.multiple_of(at, width), width)

    row_slot = pl.ds(pl.multiple_of(inner * 16, 16), 16)

    for a in range(2):
        pltpu.make_async_copy(
            (enc, dec)[a].at[:, columns(dest_inner * BLOCK, BLOCK)], rows.at[a, row_slot, :], row_r.at[a]).start()
        pltpu.make_async_copy(
            (acts, cot)[a].at[:, columns(dest_inner * BLOCK, BLOCK)], tok.at[a, 0], tok_r.at[a, 0]).start()
    idsb[0] = ids[...]

    barrier = pltpu.get_barrier_semaphore()
    for j in range(CHIPS):
        for dc in range(2):
            if j or dc:
                pl.semaphore_signal(barrier, inc=1, device_id=member(j, dc), device_id_type=MESH)
    for e in range(1, 8):
        pl.semaphore_signal(barrier, inc=1, device_id=(half + beside[e], outer), device_id_type=MESH)
    pl.semaphore_signal(barrier, inc=1, device_id=further, device_id_type=MESH)

    @pl.when(border)
    def _():
        for i in range(8):
            pl.semaphore_signal(barrier, inc=1, device_id=(8 - half + i, facing), device_id_type=MESH)

    for z1 in range(NZ):
        for x1 in range(NX):
            y1 = rem(wanted + (64 - 2 * x1 - 3 * z1), 8)
            src = ((z1 // 4) * 8 + x1 * 2 + c, y1 * 4 + z1 % 4)

            @pl.when((src[0] != inner) | (src[1] != outer))
            def _():
                pl.semaphore_signal(barrier, inc=1, device_id=src, device_id_type=MESH)

    pl.semaphore_wait(barrier, 2 * CHIPS - 1 + 8 + SOURCES + 8 * border.astype(jnp.int32) - stays.astype(jnp.int32))

    def remote(src, dst, send, recv, dev):
        return pltpu.make_async_remote_copy(
            src_ref=src, dst_ref=dst, send_sem=send, recv_sem=recv, device_id=dev, device_id_type=MESH)

    def arrived(ref, sem):
        pltpu.make_async_copy(ref, ref, sem).wait()

    others = pl.ds(1, 2 * CHIPS - 1)
    near_rows, far_rows = (pl.ds(pl.multiple_of(h, 128), 128) for h in (zh * 128, 128 - zh * 128))

    for a in range(2):
        @pl.when(border)
        def _():
            for i in range(8):
                at = rem(facing_number + 2 * (i // 2), 8) * 2 + i % 2
                remote((enc, dec)[a].at[:, columns(at * BLOCK, BLOCK)], rows.at[a, row_slot, :],
                       cross_s.at[a], cross_r.at[a], (8 - half + i, facing)).start()

        for e in range(1, 8):
            at = rem(2 * div(beside[e], 2) + y + 3 * z, 8) * 2 + rem(beside[e], 2)
            remote((enc, dec)[a].at[:, columns(at * BLOCK, BLOCK)],
                   rows.at[a, row_slot, :], row_s.at[a], row_r.at[a], (half + beside[e], outer)).start()
    for j in range(CHIPS):
        for dc in range(2):
            if j or dc:
                remote(ids, idsb.at[2 * j + dc], ids_s, ids_r, owner(j, dc)).start()
    for j in (7, 8, 0, 1, 2, 3, 4, 5, 6):
        for dc in range(2):
            at = (owner_number[j] + cs[dc]) * BLOCK
            for a in range(2):
                if j >= WHOLE:
                    h = j - WHOLE
                    remote((acts, cot)[a].at[:, columns(at + h * HALF, HALF)], tokh.at[a, h, dc],
                           half_s.at[a], half_r.at[a, h, dc], owner(j, dc)).start()
                elif j or dc:
                    remote((acts, cot)[a].at[:, columns(at, BLOCK)], tok.at[a, 2 * j + dc],
                           tok_s.at[a], tok_r.at[a, 2 * j + dc], owner(j, dc)).start()

    @pl.when(border)
    def _():
        for a in range(2):
            arrived(rows.at[a, far_rows, :], cross_r.at[a])
            remote(rows.at[a, far_rows, :], rows.at[a, far_rows, :], relay_s.at[a], cross_r.at[a], further).start()

    latent = lax.broadcasted_iota(jnp.int32, (LB, 2 * TOK), 0)

    def both(ref):
        return jnp.concatenate([ref[0], ref[1]], axis=1)

    def partials(j, left, right):
        which = both(idsb[pl.ds(2 * j, 2)])
        hits = [which[k:k + 1, :] == latent for k in range(K)]
        out = []
        for a in range(2):
            full = lax.dot_general(left(a), right(a), (((1,), (1,)), ((), ())), preferred_element_type=jnp.float32)
            for k in range(K):
                out.append(jnp.sum(jnp.where(hits[k], full, 0.0), axis=0, keepdims=True))
        out = jnp.concatenate(out, axis=0)
        pout[2 * j] = out[:, :TOK]
        pout[2 * j + 1] = out[:, TOK:]

    def send_partials(j):
        for dc in range(2):
            if j or dc:
                remote(pout.at[2 * j + dc], pin.at[2 * j + dc], p_s, p_r, member(j, dc)).start()
            else:
                pin[0] = pout[0]

    for a in range(2):
        arrived(rows.at[a, near_rows, :], row_r.at[a])

        @pl.when(jnp.logical_not(border))
        def _():
            arrived(rows.at[a, far_rows, :], cross_r.at[a])
    arrived(idsb.at[others], ids_r)

    def left(j):
        h = j - WHOLE
        return lambda a: rows[a] if j < WHOLE else rows[a, :, h * HALF:(h + 1) * HALF]

    def right(j):
        return lambda a: (tok[a, 2 * j:2 * j + 2].reshape(2 * TOK, BLOCK) if j < WHOLE else
                          tokh[a, j - WHOLE].reshape(2 * TOK, HALF))

    for group in ((0, 1, 2), (3, 4, 5), (6, 7, 8)):
        for j in group:
            for a in range(2):
                for dc in range(2):
                    if j < WHOLE:
                        arrived(tok.at[a, 2 * j + dc], tok_r.at[a, 2 * j + dc])
                    else:
                        arrived(tokh.at[a, j - WHOLE, dc], half_r.at[a, j - WHOLE, dc])
        for j in group:
            partials(j, left(j), right(j))
        for j in group:
            send_partials(j)

    for a in range(2):
        arrived(rows.at[a, pl.ds(0, LB // 2 - 16), :], row_s.at[a])

        @pl.when(border)
        def _():
            arrived(rows.at[a, far_rows, :], cross_s.at[a])
            arrived(rows.at[a, far_rows, :], relay_s.at[a])
        arrived(tok.at[a, pl.ds(1, 2 * WHOLE - 1)], tok_s.at[a])
        arrived(tokh.at[a], half_s.at[a])
    arrived(idsb.at[others], ids_s)

    arrived(pin.at[others], p_r)
    codes = jnp.sum(pin[...], axis=0)
    cout[...] = codes.astype(jnp.bfloat16).astype(jnp.float32)
    for j in range(CHIPS):
        for dc in range(2):
            if j or dc:
                remote(cout, cin.at[2 * j + dc], c_s, c_r, owner(j, dc)).start()
    cin[0] = cout[...]
    arrived(pout.at[others], p_s)
    arrived(cin.at[others], c_r)

    latent16 = latent.astype(jnp.float32).astype(jnp.bfloat16)

    for j in range(CHIPS):
        which = both(idsb[pl.ds(2 * j, 2)]).astype(jnp.float32).astype(jnp.bfloat16)
        values = both(cin[pl.ds(2 * j, 2)]).astype(jnp.bfloat16)
        hits = [which[k:k + 1, :] == latent16 for k in range(K)]
        at = pl.ds(2 * TOK * j, 2 * TOK)
        for a in range(2):
            full = jnp.zeros((LB, 2 * TOK), jnp.bfloat16)
            for k in range(K):
                full = jnp.where(hits[k], values[a * K + k:a * K + k + 1, :], full)
            spread[a, :, at] = full

    split = 2 * WHOLE * TOK

    def term(a, h):
        def product(left, right):
            return lax.dot_general(left, right, (((1,), (0,)), ((), ())), preferred_element_type=jnp.float32)

        at = split + h * 2 * TOK
        out = product(spread[1 - a, :, :split], tok[a, :, :, h * HALF:(h + 1) * HALF].reshape(split, HALF))
        out = out + product(spread[1 - a, :, at:at + 2 * TOK], tokh[a, h].reshape(2 * TOK, HALF))
        return out.reshape(SOURCES, 8, HALF)

    for h in halves:
        tsend[h] = jnp.concatenate([term(a, h) for a in range(2)], axis=1).astype(jnp.bfloat16)

        @pl.when(stays)
        def _():
            pltpu.make_async_copy(tsend.at[h, outer], fin.at[h, source], f_r.at[h]).start()

        @pl.when(jnp.logical_not(stays))
        def _():
            remote(tsend.at[h, outer], fin.at[h, source], f_s.at[h], f_r.at[h], (dest_inner, outer)).start()

        for at in dests[1:]:
            remote(tsend.at[h, at], fin.at[h, source], f_s.at[h], f_r.at[h], (dest_inner, at)).start()

    arrived(cin.at[others], c_s)
    for h in halves:
        arrived(fin.at[h], f_r.at[h])
        both_grads = jnp.sum(fin[h].astype(jnp.float32), axis=0)
        oenc[:, h * HALF:(h + 1) * HALF] = both_grads[:8]
        odec[:, h * HALF:(h + 1) * HALF] = both_grads[8:]
    for h in halves:
        @pl.when(stays)
        def _():
            arrived(tsend.at[h, pl.ds(1, SOURCES - 1)], f_s.at[h])

        @pl.when(jnp.logical_not(stays))
        def _():
            arrived(tsend.at[h], f_s.at[h])


def local(acts, cotangent, latent_ids, enc_rows, dec_rows):
    ids = latent_ids.T
    vmem, hbm = pl.BlockSpec(memory_space=pltpu.VMEM), pl.BlockSpec(memory_space=pl.ANY)
    dma = pltpu.SemaphoreType.DMA
    two = dma((2,))
    return pl.pallas_call(
        kernel,
        out_shape=(jax.ShapeDtypeStruct((8, BLOCK), jnp.float32),) * 2,
        in_specs=[hbm, hbm, vmem, hbm, hbm],
        out_specs=(vmem, vmem),
        scratch_shapes=[
            pltpu.VMEM((2, 2 * WHOLE, TOK, BLOCK), jnp.bfloat16),
            pltpu.VMEM((2, 2, 2, TOK, HALF), jnp.bfloat16),
            pltpu.VMEM((2, LB, BLOCK), jnp.bfloat16),
            pltpu.VMEM((2 * CHIPS, K, TOK), jnp.int32),
            pltpu.VMEM((2 * CHIPS, 8, TOK), jnp.float32),
            pltpu.VMEM((2 * CHIPS, 8, TOK), jnp.float32),
            pltpu.VMEM((8, TOK), jnp.float32),
            pltpu.VMEM((2 * CHIPS, 8, TOK), jnp.float32),
            pltpu.VMEM((2, LB, 2 * CHIPS * TOK), jnp.bfloat16),
            pltpu.VMEM((2, SOURCES, 16, HALF), jnp.bfloat16),
            pltpu.VMEM((2, SOURCES, 16, HALF), jnp.bfloat16),
            two, dma((2, 2 * WHOLE)), two, dma((2, 2, 2)),
            two, two, two, two, two,
            dma, dma, dma, dma, dma, dma, two, two,
        ],
        compiler_params=pltpu.CompilerParams(
            collective_id=0, has_side_effects=True, vmem_limit_bytes=60 * 2**20),
    )(acts, cotangent, ids, enc_rows, dec_rows)


def solution(mesh):
    placed = (
        P(("inner", "outer"), None),
        P(("inner", "outer"), None),
        P(("inner", "outer"), None),
        P("inner", None),
        P("inner", None),
    )
    return jax.shard_map(
        local,
        mesh=mesh,
        in_specs=placed,
        out_specs=(P("outer", "inner"), P("outer", "inner")),
        check_vma=False,
    )
```
